256 devices in a mesh: section: 4 (over x_lo, core), expert: 64 (over x_hi, z, y).
Axes of the slice: x: 4 (x_hi: 2, x_lo: 2; x = x_hi * 2 + x_lo), y: 4, z: 8, core: 2. Of those that a mesh axis runs over, the one named last changes fastest.
Arguments:
- hidden_in: bfloat16 [1, 256, 3584], P(None, 'expert'), may hold values from -6 to 6
- routes: int32 [2, 4, 1, 256, 2], P(None, 'section', None, 'expert'), may hold values from 0 to 7, all different within a row; in each aligned block of 4 rows (0 to 3, 4 to 7, ..., all dimensions but the last counted through in order) at most 2 rows name the same one
- norm_gain: float32 [2, 4, 3584], P(None, 'section'), may hold values from 0.5 to 1.5
- router_weight: bfloat16 [2, 4, 3584, 8], P(None, 'section'), may hold values from -0.09375 to 0.09375
- gate_weight: bfloat16 [2, 4, 64, 3584, 256], P(None, 'section', 'expert'), may hold values from -0.09375 to 0.09375
- up_weight: bfloat16 [2, 4, 64, 3584, 256], P(None, 'section', 'expert'), may hold values from -0.09375 to 0.09375
- down_weight: bfloat16 [2, 4, 64, 256, 3584], P(None, 'section', 'expert'), may hold values from -0.125 to 0.125
Outputs:
- hidden_out: bfloat16 [1, 256, 3584], P(None, 'expert', 'section')
The draws below stay inside these ranges and needn't reach their ends.
Inputs may be any that keep to these rules, and one draw needn't show every extreme that they name: `routes`: each row names 2 different experts. Among the 4 tokens of one block, for one layer and micro-batch, no expert is named more than 2 times, a bound that some block reaches.
All inputs are finite; a program needn't handle non-finite values.
Results may differ from the reference program's by a relative error of at most 0.04.
Values may be sent and summed in bfloat16 or wider, within the bound.
A program may use at most 64 MiB of HBM per device.

```python
import math
import jax
import jax.numpy as jnp
import numpy as np
from jax import lax

D = 3584
FF = 2048
EXP_FL = 8
TOPK = 2
MICRO = 1
TOK_DEV = 4
SPLIT = 8
HID_DEV = 256
CAP = 2
TOKENS = 256
N_SECTION = 4
N_EXPERT = 64


def block_levels(own_key, shape, shards, smallest, largest):
    level = 1.0
    for dim, shards_of in shards:
        heights = jax.random.uniform(jax.random.fold_in(jax.random.fold_in(own_key, 6), dim), (shards_of,), jnp.float32, smallest / len(shards), largest / len(shards))
        level = level * jnp.repeat(jnp.exp(heights), shape[dim] // shards_of).reshape((-1,) + (1,) * (len(shape) - 1 - dim))
    return level


def assign_block(own_key, own, number, rows, count, top, most, lean):
    order = jax.random.permutation(own_key, count)
    heavy_load, usual = shares(count, rows * top, most, lean, True), shares(count, rows * top, most, lean, False)
    places = jnp.arange(count)

    def named(tallies, offset_by):
        used = int((tallies > 0).sum())
        fixed = max(1, used // 4)
        moved = fixed + (places - fixed + offset_by * (used - fixed)) % max(1, count - fixed)
        return jnp.zeros((count,), jnp.int32).at[order[jnp.where(places < fixed, places, moved)]].set(jnp.asarray(tallies, jnp.int32))

    tallies = jnp.where(number % 4 == 0, named(heavy_load, number // 4), named(usual, number - number // 4 - 1))
    mixed = jax.random.permutation(jax.random.fold_in(own, 3), count)
    donor, receiver = mixed[0:count // 2 * 2:2], mixed[1:count // 2 * 2:2]
    room = jnp.minimum(tallies[donor] - 1, most - tallies[receiver]) // 2
    room = jnp.where((donor == order[0]) | (receiver == order[0]) | (tallies[receiver] == 0), 0, jnp.maximum(room, 0))
    moved = jax.random.randint(jax.random.fold_in(own, 4), (count // 2,), 0, 1 << 20) % (room + 1)
    tallies = tallies.at[donor].add(-moved).at[receiver].add(moved)
    labels = jnp.searchsorted(jnp.cumsum(tallies), jnp.arange(rows * top), side="right").astype(jnp.int32)
    grid = labels.reshape(top, rows).T
    grid = grid[jax.random.permutation(jax.random.fold_in(own, 1), rows)]
    offset_by = jax.random.randint(jax.random.fold_in(own, 2), (rows, 1), 0, top)
    return jnp.take_along_axis(grid, (jnp.arange(top)[None, :] + offset_by) % top, axis=1)


def shares(amount, total, limit, slope, full):
    portions = [(1 << 20) // math.isqrt(standing ** slope) + 1 for standing in range(1, amount + 1)]
    largest = limit if full else min(limit, max(-(-total // amount), total * portions[0] // sum(portions)))
    least = 1 if total - largest >= amount - 1 else 0
    given, surplus = [largest] + [least] * (amount - 1), total - largest - least * (amount - 1)
    while surplus > 0:
        candidates = [i for i in range(1, amount) if given[i] < largest] or [i for i in range(1, amount) if given[i] < limit]
        mass, budget = sum([portions[i] for i in candidates]), surplus
        for i in candidates:
            addition = min(limit - given[i], max(1, budget * portions[i] // mass), surplus)
            given[i] = given[i] + addition
            surplus = surplus - addition
    return np.array(given)


def scatter_about(own_key, extent, deviation, reach, pieces=(), held_as=jnp.bfloat16):
    entries = jax.random.normal(own_key, extent, jnp.float32) * deviation
    if len(pieces) > 0:
        entries = block_levels(own_key, extent, pieces, -0.22, 0.18) * entries
    return jnp.clip(entries, min=-reach, max=reach).astype(held_as)


def setup_inputs(seed: int = 0) -> dict:
    key_list = jax.random.split(jax.random.key(seed), 8)
    hidden_in = scatter_about(key_list[0], (MICRO, TOKENS, D), 1.0, 6.0, ((1, 64),))
    routes_keys = jax.random.split(jax.random.fold_in(key_list[1], 1), 2 * N_SECTION * MICRO * TOKENS // TOK_DEV)
    routes_turns = jax.random.permutation(jax.random.fold_in(key_list[1], 3), 2 * N_SECTION * MICRO * TOKENS // TOK_DEV)
    routes = jax.vmap(lambda own, number: assign_block(jax.random.fold_in(key_list[1], 2), own, number, TOK_DEV, EXP_FL, TOPK, CAP, 2))(routes_keys, routes_turns).reshape((2, N_SECTION, MICRO, TOKENS, TOPK))
    norm_gain = jnp.clip(1.0 + 0.1 * jax.random.normal(key_list[2], (2, N_SECTION, D), jnp.float32), 0.5, 1.5)
    router_weight = scatter_about(key_list[3], (2, N_SECTION, D, EXP_FL), D ** -0.5, 0.09375, ((1, 4),))
    gate_weight = scatter_about(key_list[4], (2, N_SECTION, N_EXPERT, D, HID_DEV), D ** -0.5, 0.09375, ((1, 4), (2, 64)))
    up_weight = scatter_about(key_list[5], (2, N_SECTION, N_EXPERT, D, HID_DEV), D ** -0.5, 0.09375, ((1, 4), (2, 64)))
    down_weight = scatter_about(key_list[6], (2, N_SECTION, N_EXPERT, HID_DEV, D), FF ** -0.5, 0.125, ((1, 4), (2, 64)))
    return {"hidden_in": hidden_in, "routes": routes, "norm_gain": norm_gain, "router_weight": router_weight, "gate_weight": gate_weight, "up_weight": up_weight, "down_weight": down_weight}


def layer_reference(current, gain, router, w_gate, w_up, w_down, layer_routes):
    blocks = current.reshape(N_EXPERT, TOK_DEV, D)
    widened = blocks.astype(jnp.float32)
    mean_square = lax.optimization_barrier(jnp.mean(widened * widened, axis=-1, keepdims=True))
    normalized = (widened * lax.rsqrt(mean_square + 1e-06) * gain[None, None, :]).astype(jnp.bfloat16)
    router_logits = jnp.einsum('btd,de->bte', normalized.astype(jnp.float32), router.astype(jnp.float32))
    affinity = jax.nn.sigmoid(router_logits)
    block_routes = layer_routes.reshape(N_EXPERT, TOK_DEV, TOPK).astype(jnp.int32)
    expert_ids = jnp.arange(EXP_FL, dtype=jnp.int32)
    picked_onehot = (block_routes[..., None] == expert_ids).astype(jnp.int32)
    chosen_affinity = lax.optimization_barrier(jnp.sum(picked_onehot.astype(jnp.float32) * affinity[:, :, None, :], axis=-1))
    mix_weights = 2.5 * chosen_affinity / lax.optimization_barrier(jnp.sum(chosen_affinity, axis=-1, keepdims=True))
    flat_onehot = picked_onehot.reshape(N_EXPERT, TOK_DEV * TOPK, EXP_FL)
    earlier_count = jnp.cumsum(flat_onehot, axis=1) - flat_onehot
    slot_index = lax.optimization_barrier(jnp.sum(earlier_count * flat_onehot, axis=-1)).astype(jnp.int32)
    buffer_pos = block_routes.reshape(N_EXPERT, TOK_DEV * TOPK) * CAP + slot_index
    slot_ids = jnp.arange(EXP_FL * CAP, dtype=jnp.int32)
    slot_select = (buffer_pos[..., None] == slot_ids).astype(jnp.float32).reshape(N_EXPERT, TOK_DEV, TOPK, EXP_FL * CAP)
    place_matrix = lax.optimization_barrier(jnp.sum(slot_select, axis=2))
    mix_matrix = lax.optimization_barrier(jnp.sum(slot_select * mix_weights[..., None], axis=2))
    outgoing = jnp.einsum('btp,btd->bpd', place_matrix, normalized.astype(jnp.float32)).astype(jnp.bfloat16)
    per_expert = outgoing.reshape(N_EXPERT, EXP_FL, CAP, D).transpose(1, 0, 2, 3).reshape(EXP_FL, N_EXPERT * CAP, D)
    gate_slices = w_gate.reshape(EXP_FL, SPLIT, D, HID_DEV)
    up_slices = w_up.reshape(EXP_FL, SPLIT, D, HID_DEV)
    down_slices = w_down.reshape(EXP_FL, SPLIT, HID_DEV, D)

    def one_expert(operands):
        expert_rows, gates, ups, downs = operands

        def add_slice(total, slice_weights):
            gate_part, up_part, down_part = slice_weights
            gate_acts = jnp.dot(expert_rows, gate_part, preferred_element_type=jnp.float32)
            up_acts = jnp.dot(expert_rows, up_part, preferred_element_type=jnp.float32)
            hidden_acts = (jax.nn.silu(gate_acts) * up_acts).astype(jnp.bfloat16)
            partial_out = jnp.dot(hidden_acts, down_part, preferred_element_type=jnp.float32).astype(jnp.bfloat16)
            partial_out = lax.optimization_barrier(partial_out)
            return (total + partial_out.astype(jnp.float32), None)
        start_total = jnp.zeros((N_EXPERT * CAP, D), jnp.float32)
        total, unused = lax.scan(add_slice, start_total, (gates, ups, downs))
        return total
    expert_out = lax.map(one_expert, (per_expert, gate_slices, up_slices, down_slices))
    expert_out = expert_out.reshape(EXP_FL, N_EXPERT, CAP, D).transpose(1, 0, 2, 3).reshape(N_EXPERT, EXP_FL * CAP, D)
    routed_sum = jnp.einsum('btp,bpd->btd', mix_matrix, expert_out, precision=lax.Precision.HIGHEST)
    return (widened + routed_sum).astype(jnp.bfloat16).reshape(TOKENS, D)

def reference(hidden_in, routes, norm_gain, router_weight, gate_weight, up_weight, down_weight):
    layer_order = [(0, section_pos) for section_pos in range(N_SECTION)] + [(1, section_pos) for section_pos in reversed(range(N_SECTION))]
    results = []
    for micro_index in range(MICRO):
        current = hidden_in[micro_index]
        for half_index, section_pos in layer_order:
            current = layer_reference(current, norm_gain[half_index, section_pos], router_weight[half_index, section_pos], gate_weight[half_index, section_pos], up_weight[half_index, section_pos], down_weight[half_index, section_pos], routes[half_index, section_pos, micro_index])
        results.append(current)
    return jnp.stack(results)
```

```python
import functools

import jax
import jax.numpy as jnp
from jax import lax
from jax.experimental import pallas as pl
from jax.experimental.pallas import tpu as pltpu
from jax.sharding import PartitionSpec as P

MESH = pl.DeviceIdType.MESH
F32 = jnp.float32
BF16 = jnp.bfloat16

OWNER = 2
D = 3584
CH = 896
HID = 256
EXPERTS = 8
ROWS = 8
SET = 16
STEPS = 8
GROUPS = 4
PER = EXPERTS // GROUPS


def remote(src, dst, send, recv, section, expert):
    return pltpu.make_async_remote_copy(
        src_ref=src,
        dst_ref=dst,
        send_sem=send,
        recv_sem=recv,
        device_id=(section, expert),
        device_id_type=MESH,
    )


def wait_for(ref, sem):
    pltpu.make_async_copy(ref, ref, sem).wait()


def iota(shape, dim):
    return lax.broadcasted_iota(jnp.int32, shape, dim)


def kernel(
    hidden_hbm, routes_hbm, gain_hbm, router_hbm, gate_hbm, up_hbm, down_hbm, out_ref,
    hid_v, routes_v, gain_v, router_v, gate_v, up_v, down_v,
    rt_out, rt_in, rsum, hx_out, hx_in, pt, x_v, disp, xb, sb, rb, aff_v, pb, ro,
    fin_out, fin_in,
    in_sem, w_sem, rt_send, rt_recv, hx_send, hx_recv, d_send, d_recv, g_send, g_recv,
    r_send, r_recv, c_send, c_recv, f_send, f_recv,
):
    s = lax.axis_index("section")
    i = lax.axis_index("expert")
    xh = i // 32
    z = (i // 4) % 8
    y = i % 4
    zp = z % 2
    e = i // 8
    me8 = i % 8
    base8 = i - me8
    base4 = i - y
    is_owner = s == OWNER

    def y_at(k):
        return (y + k) % 4

    def member(zr, k):
        return ((zp + zr) % 2) * 4 + y_at(k)

    def to_live(j, xf):
        up = (z + j) % 2 == 0
        zd = jnp.where(up, (z + j) % 8, (z - j + 8) % 8)
        xd = (xh + xf) % 2
        return xd, zd

    def to_owner(j, xf):
        zo = jnp.where(zp == 0, (z - j + 8) % 8, (z + j) % 8)
        xd = (xh + xf) % 2
        return xd * 32 + zo * 4 + y

    small = [
        pltpu.make_async_copy(hidden_hbm, hid_v, in_sem.at[0]),
        pltpu.make_async_copy(routes_hbm, routes_v, in_sem.at[1]),
    ]
    for copy in small:
        copy.start()

    def weights(c):
        return [
            pltpu.make_async_copy(gain_hbm.at[c], gain_v.at[c], w_sem.at[c, 0]),
            pltpu.make_async_copy(router_hbm.at[c], router_v.at[c], w_sem.at[c, 1]),
            pltpu.make_async_copy(gate_hbm.at[c, 0, 0], gate_v.at[c], w_sem.at[c, 2]),
            pltpu.make_async_copy(up_hbm.at[c, 0, 0], up_v.at[c], w_sem.at[c, 3]),
            pltpu.make_async_copy(down_hbm.at[c, 0, 0], down_v.at[c], w_sem.at[c, 4]),
        ]

    for c in range(2):
        for copy in weights(c):
            copy.start()

    barrier = pltpu.get_barrier_semaphore()

    def greet(section, expert):
        pl.semaphore_signal(barrier, inc=1, device_id=(section, expert), device_id_type=MESH)

    for k in range(1, 8):
        greet(s, base8 + (me8 + k) % 8)
    for k in range(1, 4):
        greet(OWNER, base4 + y_at(k))
    for j in range(4):
        for xf in range(2):
            if j == 0 and xf == 0:
                @pl.when(jnp.logical_not(is_owner))
                def _():
                    greet(OWNER, to_owner(0, 0))
            else:
                greet(OWNER, to_owner(j, xf))

    @pl.when(is_owner)
    def _():
        for sec in range(4):
            for k in range(1, 4):
                greet(sec, base4 + y_at(k))
            for j in range(4):
                for xf in range(2):
                    if sec == OWNER and j == 0 and xf == 0:
                        continue
                    xd, zd = to_live(j, xf)
                    greet(sec, xd * 32 + zd * 4 + y)
        pl.semaphore_wait(barrier, 60)

    @pl.when(jnp.logical_not(is_owner))
    def _():
        pl.semaphore_wait(barrier, 18)

    for copy in small:
        copy.wait()
    place = (iota((SET, 4), 0) == 4 * y + iota((SET, 4), 1)).astype(BF16)
    lane = iota((4, 128), 1)
    tile = jnp.zeros((4, 128), F32)
    for c in range(2):
        chosen = routes_v[c, 0, 0].astype(F32)
        for k in range(2):
            tile = tile + jnp.where(lane == 2 * c + k, chosen[:, k : k + 1], 0.0)
    rt_out[...] = jnp.dot(place, tile.astype(BF16), preferred_element_type=F32)

    @pl.when(is_owner)
    def _():
        placed = jnp.dot(place, hid_v[0], preferred_element_type=F32).astype(BF16)
        for k in range(4):
            hx_out[k] = placed[:, k * CH : (k + 1) * CH]
        for k in range(1, 4):
            remote(
                hx_out.at[y_at(k)], hx_in.at[y], hx_send.at[k], hx_recv.at[y],
                s, base4 + y_at(k),
            ).start()

    for k in range(1, 4):
        remote(
            rt_out, rt_in.at[s, y], rt_send.at[k], rt_recv.at[s, y], OWNER, base4 + y_at(k)
        ).start()

    @pl.when(jnp.logical_not(is_owner))
    def _():
        remote(
            rt_out, rt_in.at[s, y], rt_send.at[0], rt_recv.at[s, y], OWNER, i
        ).start()

    def live_of(step):
        return jnp.where(step < 4, step, 7 - step)

    def make_pt(step):
        half = step // 4
        routes = rsum[live_of(step)]
        lanes = iota((SET, 128), 1)
        first = jnp.sum(jnp.where(lanes == 2 * half, routes, 0.0), axis=1, keepdims=True)
        second = jnp.sum(jnp.where(lanes == 2 * half + 1, routes, 0.0), axis=1, keepdims=True)
        slots = iota((SET, 64), 1)
        token = iota((SET, 64), 0)
        expert = (slots // 8).astype(F32)
        named = jnp.logical_or(first == expert, second == expert)
        onehot = jnp.where(named, 1.0, 0.0)
        row = iota((SET, SET), 0)
        col = iota((SET, SET), 1)
        earlier = jnp.logical_and(row // 4 == col // 4, col < row)
        count = jnp.dot(
            jnp.where(earlier, 1.0, 0.0).astype(BF16), onehot.astype(BF16),
            preferred_element_type=F32,
        )
        fits = jnp.logical_and(
            count == (slots % 2).astype(F32), (slots % 8) // 2 == token // 4
        )
        pt[step] = jnp.where(jnp.logical_and(named, fits), 1.0, 0.0).astype(BF16)

    @pl.when(is_owner)
    def _():
        rt_in[OWNER, y] = rt_out[...]
        for k in range(1, 4):
            wait_for(hx_in.at[y_at(k)], hx_recv.at[y_at(k)])
        hx_in[y] = hx_out[y]
        x = jnp.zeros((SET, CH), F32)
        for k in range(4):
            x = x + hx_in[k].astype(F32)
        x_v[...] = x
        for sec in range(4):
            for k in range(4):
                if k == 0 and sec == OWNER:
                    continue
                wait_for(rt_in.at[sec, y_at(k)], rt_recv.at[sec, y_at(k)])
            total = jnp.zeros((SET, 128), F32)
            for k in range(4):
                total = total + rt_in[sec, k]
            rsum[sec] = total
        make_pt(0)

    def combine(step):
        for k in range(EXPERTS):
            wait_for(ro.at[k], c_recv.at[k])
        rows = ro[...].astype(F32).reshape(EXPERTS * ROWS, CH + 128).astype(BF16)
        mixed = jnp.dot(pt[step], rows, preferred_element_type=F32)
        weight = mixed[:, CH : CH + 1] + mixed[:, CH + 1 : CH + 2]
        fresh = x_v[...] + 2.5 * mixed[:, :CH] / weight
        x_v[...] = fresh.astype(BF16).astype(F32)

    def owner_step(step):
        live = live_of(step)
        half = step // 4

        @pl.when(step > 0)
        def _():
            combine(step - 1)
            for m in range(1, 8):
                wait_for(disp.at[m], d_send.at[m])

            @pl.when(live_of(step - 1) != OWNER)
            def _():
                wait_for(disp.at[0], d_send.at[0])

        rows = lax.dot_general(
            pt[step], x_v[...].astype(BF16), (((0,), (0,)), ((), ())),
            preferred_element_type=F32,
        )
        disp[...] = rows.reshape(EXPERTS, ROWS, CH).astype(BF16)
        for j in (3, 2, 1, 0):
            for xf in (1, 0):
                m = 2 * j + xf
                xd, zd = to_live(j, xf)
                src = disp.at[xd * 4 + zd // 2]
                dst = xb.at[half, y, zd % 2, m]

                def send():
                    remote(
                        src, dst, d_send.at[m], d_recv.at[half, m], live, xd * 32 + zd * 4 + y
                    ).start()

                if m > 0:
                    send()
                else:
                    pl.when(live != OWNER)(send)

                    @pl.when(live == OWNER)
                    def _():
                        pltpu.make_async_copy(src, dst, d_recv.at[half, m]).start()

        @pl.when(step < STEPS - 1)
        def _():
            make_pt(step + 1)

    others = [(1, 2), (1, 1), (1, 3), (0, 2), (0, 1), (0, 3), (1, 0)]

    def live_step(half):
        for part in reversed(range(GROUPS)):
            for m in range(part * PER, (part + 1) * PER):
                wait_for(xb.at[half, y, zp, m], d_recv.at[half, m])
            rows = xb.at[half, y, zp, pl.ds(part * PER, PER)]
            for n, (zr, k) in enumerate(others):
                remote(
                    rows, rows, g_send.at[n, part], g_recv.at[half, me8, part],
                    s, base8 + member(zr, k),
                ).start()
        for copy in weights(half):
            copy.wait()
        gate = jnp.zeros((128, HID), F32)
        up = jnp.zeros((128, HID), F32)
        logits = jnp.zeros((128, EXPERTS), F32)
        squares = jnp.zeros((128, 1), F32)
        for k in (0, 1, 3, 2):
            yk = y_at(k)
            for zr in range(2):
                if zr == 0 and k == 0:
                    continue
                for part in range(GROUPS):
                    wait_for(
                        xb.at[half, yk, (zp + zr) % 2, pl.ds(part * PER, PER)],
                        g_recv.at[half, member(zr, k), part],
                    )
            rows = xb[half, yk].astype(F32).reshape(128, CH)
            squares = squares + jnp.sum(rows * rows, axis=1, keepdims=True)
            start = pl.multiple_of(yk * CH, 128)
            scaled = (rows * gain_v[half, :, pl.ds(start, CH)]).astype(BF16)
            depth = pl.ds(start, CH)
            gate = gate + jnp.dot(scaled, gate_v[half, depth, :], preferred_element_type=F32)
            up = up + jnp.dot(scaled, up_v[half, depth, :], preferred_element_type=F32)
            logits = logits + jnp.dot(
                scaled, router_v[half, 0, depth, :], preferred_element_type=F32
            )
        scale = lax.rsqrt(squares * (1.0 / D) + 1e-06)
        gate = gate * scale
        act = (gate * jax.nn.sigmoid(gate) * (up * scale)).astype(BF16)
        own = jnp.where(iota((128, EXPERTS), 1) == e, logits, 0.0)
        affinity = jax.nn.sigmoid(jnp.sum(own, axis=1, keepdims=True) * scale)
        aff_v[...] = jnp.broadcast_to(affinity, (128, 128))

        for k in (2, 1, 3, 0):
            yk = y_at(k)
            cols = pl.ds(pl.multiple_of(yk * CH, 128), CH)
            piece = jnp.dot(act, down_v[half, :, cols], preferred_element_type=F32)
            sb[yk] = piece.astype(BF16).reshape(2, 64, CH)
            for zr in (1, 0):
                if zr == 0 and k == 0:
                    continue
                n = others.index((zr, k))
                remote(
                    sb.at[yk, (zp + zr) % 2], rb.at[half, me8], r_send.at[n],
                    r_recv.at[half, me8], s, base8 + member(zr, k),
                ).start()
        total = sb[y, zp].astype(F32)
        for zr, k in reversed(others):
            src = member(zr, k)
            wait_for(rb.at[half, src], r_recv.at[half, src])
            total = total + rb[half, src].astype(F32)
        mine = aff_v[pl.ds(pl.multiple_of(zp * 64, 64), 64), :]
        pb[:, :, :CH] = (total * mine[:, :1]).reshape(EXPERTS, ROWS, CH).astype(BF16)
        high = mine.astype(BF16).astype(F32)
        lanes = iota((64, 128), 1)
        extra = jnp.where(lanes == 0, high, jnp.where(lanes == 1, mine - high, 0.0))
        pb[:, :, CH:] = extra.reshape(EXPERTS, ROWS, 128).astype(BF16)
        for j in (3, 2, 1, 0):
            for xf in (1, 0):
                m = 2 * j + xf

                def send():
                    remote(
                        pb.at[m], ro.at[e], c_send.at[m], c_recv.at[e], OWNER, to_owner(j, xf)
                    ).start()

                if m > 0:
                    send()
                else:
                    pl.when(jnp.logical_not(is_owner))(send)

                    @pl.when(is_owner)
                    def _():
                        pltpu.make_async_copy(pb.at[m], ro.at[e], c_recv.at[e]).start()

        for n, (zr, k) in enumerate(others):
            for part in range(GROUPS):
                wait_for(xb.at[half, y, zp, pl.ds(part * PER, PER)], g_send.at[n, part])
            wait_for(sb.at[0, 0], r_send.at[n])
        for m in range(1, 8):
            wait_for(pb.at[m], c_send.at[m])

        @pl.when(jnp.logical_not(is_owner))
        def _():
            wait_for(pb.at[0], c_send.at[0])

    def one_step(step, carry):
        pl.when(is_owner)(lambda: owner_step(step))
        pl.when(s == live_of(step))(lambda: live_step(step // 4))
        return carry

    lax.fori_loop(0, STEPS, one_step, 0)

    @pl.when(is_owner)
    def _():
        combine(STEPS - 1)
        for m in range(8):
            wait_for(disp.at[m], d_send.at[m])
        fin_out[...] = x_v[...].astype(BF16)
        for k in range(4):
            def send():
                remote(fin_out, fin_in, f_send.at[k], f_recv, y, base4 + y_at(k)).start()

            if k > 0:
                send()
            else:
                pl.when(y != OWNER)(send)

                @pl.when(y == OWNER)
                def _():
                    pltpu.make_async_copy(fin_out, fin_in, f_recv).start()

    wait_for(fin_in, f_recv)
    pick = (iota((8, SET), 1) == 4 * y + iota((8, SET), 0)).astype(BF16)
    picked = jnp.dot(pick, fin_in[...], preferred_element_type=F32)
    out_ref[...] = picked[:4].astype(BF16)

    @pl.when(is_owner)
    def _():
        for k in range(1, 4):
            wait_for(fin_out, f_send.at[k])
            wait_for(hx_out.at[0], hx_send.at[k])

        @pl.when(y != OWNER)
        def _():
            wait_for(fin_out, f_send.at[0])

    @pl.when(jnp.logical_not(is_owner))
    def _():
        wait_for(rt_out, rt_send.at[0])

    for k in range(1, 4):
        wait_for(rt_out, rt_send.at[k])


def shards(hidden_in, routes, norm_gain, router_weight, gate_weight, up_weight, down_weight):
    dma = pltpu.SemaphoreType.DMA
    any_space = pl.BlockSpec(memory_space=pl.ANY)
    out = pl.pallas_call(
        kernel,
        out_shape=jax.ShapeDtypeStruct((4, CH), BF16),
        in_specs=[any_space] * 7,
        out_specs=pl.BlockSpec(memory_space=pltpu.VMEM),
        scratch_shapes=[
            pltpu.VMEM(hidden_in.shape, BF16),
            pltpu.VMEM(routes.shape, jnp.int32),
            pltpu.VMEM(norm_gain.shape, F32),
            pltpu.VMEM(router_weight.shape, BF16),
            pltpu.VMEM((2, D, HID), BF16),
            pltpu.VMEM((2, D, HID), BF16),
            pltpu.VMEM((2, HID, D), BF16),
            pltpu.VMEM((SET, 128), F32),
            pltpu.VMEM((4, 4, SET, 128), F32),
            pltpu.VMEM((4, SET, 128), F32),
            pltpu.VMEM((4, SET, CH), BF16),
            pltpu.VMEM((4, SET, CH), BF16),
            pltpu.VMEM((STEPS, SET, 64), BF16),
            pltpu.VMEM((SET, CH), F32),
            pltpu.VMEM((EXPERTS, ROWS, CH), BF16),
            pltpu.VMEM((2, 4, 2, EXPERTS, ROWS, CH), BF16),
            pltpu.VMEM((4, 2, 64, CH), BF16),
            pltpu.VMEM((2, 8, 64, CH), BF16),
            pltpu.VMEM((128, 128), F32),
            pltpu.VMEM((EXPERTS, ROWS, CH + 128), BF16),
            pltpu.VMEM((EXPERTS, ROWS, CH + 128), BF16),
            pltpu.VMEM((SET, CH), BF16),
            pltpu.VMEM((SET, CH), BF16),
            dma((2,)),
            dma((2, 5)),
            dma((4,)),
            dma((4, 4)),
            dma((4,)),
            dma((4,)),
            dma((8,)),
            dma((2, 8)),
            dma((7, GROUPS)),
            dma((2, 8, GROUPS)),
            dma((7,)),
            dma((2, 8)),
            dma((8,)),
            dma((8,)),
            dma((4,)),
            dma,
        ],
        compiler_params=pltpu.CompilerParams(
            collective_id=0, has_side_effects=True, vmem_limit_bytes=48 << 20
        ),
    )(hidden_in, routes, norm_gain, router_weight, gate_weight, up_weight, down_weight)
    return out[None]


def solution(mesh):
    return jax.shard_map(
        shards,
        mesh=mesh,
        in_specs=(
            P(None, "expert", None),
            P(None, "section", None, "expert", None),
            P(None, "section", None),
            P(None, "section", None, None),
            P(None, "section", "expert", None, None),
            P(None, "section", "expert", None, None),
            P(None, "section", "expert", None, None),
        ),
        out_specs=P(None, "expert", "section"),
        check_vma=False,
    )
```

```python
import jax
import jax.numpy as jnp
from jax import lax
from jax.experimental import pallas as pl
from jax.experimental.pallas import tpu as pltpu
from jax.sharding import PartitionSpec as P

MESH = pl.DeviceIdType.MESH
F32 = jnp.float32
BF16 = jnp.bfloat16

D = 3584
CH = 896
WIDE = CH + 128
HID = 256
EXPERTS = 8
ROWS = 8
SET = 16
STEPS = 8
FIRST = 3
SECOND = 0
AWAY = (4, 3, -3, 2, -2, 1, -1, 0)
FAR = 3
NEAR = len(AWAY) - FAR
FAR_SLOTS = 2 * FAR
SLOTS = FAR_SLOTS + 8 * NEAR
FAR_ROWS = 16 * FAR


def remote(src, dst, send, recv, section, expert):
    return pltpu.make_async_remote_copy(
        src_ref=src,
        dst_ref=dst,
        send_sem=send,
        recv_sem=recv,
        device_id=(section, expert),
        device_id_type=MESH,
    )


def wait_for(ref, sem):
    pltpu.make_async_copy(ref, ref, sem).wait()


def iota(shape, dim):
    return lax.broadcasted_iota(jnp.int32, shape, dim)


def kernel(
    hidden_hbm, routes_hbm, gain_hbm, router_hbm, gate_hbm, up_hbm, down_hbm, out_ref,
    hid_v, routes_v, gain_v, router_v, gate_v, up_v, down_v,
    rt_out, rt_in, rsum, hx_out, hx_in, place_pt, mix_pt, x_v, x_out, x_in, disp, xb,
    sb, rb, aff_v, near_out, far_out, ro, fin_out, fin_in,
    in_sem, w_sem, rt_send, rt_recv, hx_send, hx_recv, x_send, x_recv, d_send, a_recv,
    g_send, r_send, r_recv, n_send, c_send, c_recv, f_send, f_recv,
):
    s = lax.axis_index("section")
    i = lax.axis_index("expert")
    xh = i // 32
    z = (i // 4) % 8
    y = i % 4
    base4 = i - y
    is_first = s == FIRST
    is_second = s == SECOND

    def y_at(k):
        return (y + k) % 4

    def column(xf, away):
        return ((xh + xf) % 2) * 32 + ((z + away + 8) % 8) * 4

    def expert_at(xf, away):
        return ((xh + xf) % 2) * 4 + ((z + away + 8) % 8) // 2

    small = [
        pltpu.make_async_copy(hidden_hbm, hid_v, in_sem.at[0]),
        pltpu.make_async_copy(routes_hbm, routes_v, in_sem.at[1]),
    ]
    for copy in small:
        copy.start()

    def weights(c):
        return [
            pltpu.make_async_copy(gain_hbm.at[c], gain_v.at[c], w_sem.at[c, 0]),
            pltpu.make_async_copy(router_hbm.at[c], router_v.at[c], w_sem.at[c, 1]),
            pltpu.make_async_copy(gate_hbm.at[c, 0, 0], gate_v.at[c], w_sem.at[c, 2]),
            pltpu.make_async_copy(up_hbm.at[c, 0, 0], up_v.at[c], w_sem.at[c, 3]),
            pltpu.make_async_copy(down_hbm.at[c, 0, 0], down_v.at[c], w_sem.at[c, 4]),
        ]

    for c in range(2):
        for copy in weights(c):
            copy.start()

    barrier = pltpu.get_barrier_semaphore()

    def greet(section, expert):
        pl.semaphore_signal(barrier, inc=1, device_id=(section, expert), device_id_type=MESH)

    def greet_all(section, sign):
        for n, away in enumerate(AWAY):
            for xf in range(2):
                for k in range(1 if n < FAR else 4):
                    greet(section, column(xf, sign * away) + y_at(k))

    for k in range(1, 4):
        greet(s, base4 + y_at(k))
    pl.when(s != FIRST)(lambda: greet_all(FIRST, 1))
    pl.when(s != SECOND)(lambda: greet_all(SECOND, 1))
    pairs = 2 * FAR + 8 * NEAR

    @pl.when(jnp.logical_or(is_first, is_second))
    def _():
        lowest = jnp.where(is_first, 0, 1)
        for n in range(3):
            greet_all(lowest + n, -1)
        pl.semaphore_wait(barrier, 3 + 4 * pairs)

    @pl.when(jnp.logical_not(jnp.logical_or(is_first, is_second)))
    def _():
        pl.semaphore_wait(barrier, 3 + 2 * pairs)

    for copy in small:
        copy.wait()
    place = (iota((SET, 4), 0) == 4 * y + iota((SET, 4), 1)).astype(BF16)

    @pl.when(is_first)
    def _():
        placed = jnp.dot(place, hid_v[0], preferred_element_type=F32).astype(BF16)
        for k in range(4):
            hx_out[k] = placed[:, k * CH : (k + 1) * CH]
        for k in (2, 1, 3):
            remote(
                hx_out.at[y_at(k)], hx_in.at[y], hx_send.at[k], hx_recv.at[y],
                s, base4 + y_at(k),
            ).start()

    lane = iota((4, 128), 1)
    diagonal = iota((4, 4), 0) == iota((4, 4), 1)
    tile = jnp.zeros((4, 128), F32)
    for c in range(2):
        chosen = routes_v[c, 0, 0].astype(F32)
        for k in range(2):
            column_k = jnp.sum(jnp.where(diagonal, chosen[k : k + 1], 0.0), axis=1, keepdims=True)
            tile = tile + jnp.where(lane == 2 * c + k, column_k, 0.0)
    rt_out[...] = jnp.dot(place, tile.astype(BF16), preferred_element_type=F32)

    def send_routes(n, holder, k):
        remote(
            rt_out, rt_in.at[s, y], rt_send.at[n, k], rt_recv.at[s, y],
            holder, base4 + y_at(k),
        ).start()

    for n, holder in enumerate((FIRST, SECOND)):
        for k in range(1, 4):
            send_routes(n, holder, k)
        pl.when(s != holder)(lambda: send_routes(n, holder, 0))
        @pl.when(s == holder)
        def _():
            rt_in[holder, y] = rt_out[...]

    def gather_routes(sec):
        for k in range(1, 4):
            wait_for(rt_in.at[sec, y_at(k)], rt_recv.at[sec, y_at(k)])
        pl.when(s != sec)(lambda: wait_for(rt_in.at[sec, y], rt_recv.at[sec, y]))
        total = jnp.zeros((SET, 128), F32)
        for k in range(4):
            total = total + rt_in[sec, k]
        rsum[sec] = total

    def live_of(step):
        return jnp.where(step < 4, step, 7 - step)

    def placement(step, expert, row):
        half = step // 4
        routes = rsum[live_of(step)]
        lanes = iota((SET, 128), 1)
        one = jnp.sum(jnp.where(lanes == 2 * half, routes, 0.0), axis=1, keepdims=True)
        two = jnp.sum(jnp.where(lanes == 2 * half + 1, routes, 0.0), axis=1, keepdims=True)
        expert = expert.astype(F32)
        named = jnp.logical_or(one == expert, two == expert)
        onehot = jnp.where(named, 1.0, 0.0)
        token = iota((SET, SET), 0)
        other = iota((SET, SET), 1)
        earlier = jnp.logical_and(token // 4 == other // 4, other < token)
        count = jnp.dot(
            jnp.where(earlier, 1.0, 0.0).astype(BF16), onehot.astype(BF16),
            preferred_element_type=F32,
        )
        fits = jnp.logical_and(
            count == (row % 2).astype(F32), row // 2 == iota(row.shape, 0) // 4
        )
        return jnp.where(jnp.logical_and(named, fits), 1.0, 0.0).astype(BF16)

    def make_place(step):
        at = iota((SET, EXPERTS * ROWS), 1)
        place_pt[step] = placement(step, at // ROWS, at % ROWS)

    def make_mix(step):
        at = iota((SET, SLOTS * ROWS), 1)
        slot = at // ROWS
        near = slot >= FAR_SLOTS
        pair = jnp.where(near, FAR_SLOTS + (slot - FAR_SLOTS) // 4, slot)
        n = pair // 2
        away = jnp.zeros(at.shape, jnp.int32)
        for m, value in enumerate(AWAY):
            away = jnp.where(n == m, value, away)
        expert = ((xh + pair % 2) % 2) * 4 + ((z - away + 8) % 8) // 2
        mix_pt[step] = placement(step, expert, at % ROWS)

    def make_all():
        def body(step, carry):
            make_place(step)
            make_mix(step)
            return carry

        lax.fori_loop(0, STEPS, body, 0)

    @pl.when(is_first)
    def _():
        gather_routes(0)
        make_place(0)
        for k in range(1, 4):
            wait_for(hx_in.at[y_at(k)], hx_recv.at[y_at(k)])
        hx_in[y] = hx_out[y]
        x = jnp.zeros((SET, CH), F32)
        for k in range(4):
            x = x + hx_in[k].astype(F32)
        x_v[...] = x

    def combine(step):
        for k in range(SLOTS):
            wait_for(ro.at[k], c_recv.at[k])
        rows = ro[...].astype(F32).reshape(SLOTS * ROWS, WIDE).astype(BF16)
        mixed = jnp.dot(mix_pt[step], rows, preferred_element_type=F32)
        weight = mixed[:, CH : CH + 1] + mixed[:, CH + 1 : CH + 2]
        fresh = x_v[...] + 20.0 * mixed[:, :CH] / weight
        x_v[...] = fresh.astype(BF16).astype(F32)

    def sends(n):
        if n < FAR:
            return [(xf, 0, 2 * n + xf) for xf in (1, 0)]
        return [
            (xf, k, FAR_SLOTS + (2 * (n - FAR) + xf) * 4 + k) for k in (2, 1, 3, 0) for xf in (1, 0)
        ]

    def wait_dispatch():
        for m in range(SLOTS):
            wait_for(disp.at[0], d_send.at[m])

    def holder_step(step):
        half = step // 4

        @pl.when(jnp.logical_or(step == 2, step == 6))
        def _():
            wait_for(x_in, x_recv)
            x_v[...] = x_in[...].astype(F32)

        pl.when(step > 0)(lambda: combine(step - 1))
        pl.when(jnp.logical_and(step != 0, step != 2))(wait_dispatch)
        x_out[...] = x_v[...].astype(BF16)
        rows = lax.dot_general(
            place_pt[step], x_out[...], (((0,), (0,)), ((), ())), preferred_element_type=F32
        )
        disp[...] = rows.reshape(EXPERTS, ROWS, CH).astype(BF16)
        for n, away in enumerate(AWAY):
            for xf, k, m in sends(n):
                remote(
                    disp.at[expert_at(xf, -away)], xb.at[half, y, n, xf],
                    d_send.at[m], a_recv.at[half, y, n],
                    live_of(step), column(xf, -away) + y_at(k),
                ).start()

        @pl.when(jnp.logical_or(step == 1, step == 5))
        def _():
            handed = remote(x_out, x_in, x_send, x_recv, FIRST + SECOND - s, i)
            handed.start()
            handed.wait_send()

        @pl.when(step == 0)
        def _():
            for sec in range(1, 4):
                gather_routes(sec)
            make_all()

    def live_step(half, holder):
        for n in reversed(range(FAR)):
            rows = xb.at[half, y, n]
            wait_for(rows, a_recv.at[half, y, n])
            for k in (2, 1, 3):
                remote(
                    rows, rows, g_send.at[n, k], a_recv.at[half, y, n], s, base4 + y_at(k)
                ).start()
        for copy in weights(half):
            copy.wait()
        gate = jnp.zeros((128, HID), F32)
        up = jnp.zeros((128, HID), F32)
        logits = jnp.zeros((128, EXPERTS), F32)
        squares = jnp.zeros((128, 1), F32)
        for k in (0, 1, 3, 2):
            yk = y_at(k)
            for n in range(FAR if k == 0 else 0, len(AWAY)):
                wait_for(xb.at[half, yk, n], a_recv.at[half, yk, n])
            rows = xb[half, yk].astype(F32).reshape(128, CH)
            squares = squares + jnp.sum(rows * rows, axis=1, keepdims=True)
            start = pl.multiple_of(yk * CH, 128)
            depth = pl.ds(start, CH)
            scaled = (rows * gain_v[half, :, depth]).astype(BF16)
            gate = gate + jnp.dot(scaled, gate_v[half, depth, :], preferred_element_type=F32)
            up = up + jnp.dot(scaled, up_v[half, depth, :], preferred_element_type=F32)
            logits = logits + lax.dot_general(
                scaled, router_v[half, 0, :, depth], (((1,), (1,)), ((), ())),
                preferred_element_type=F32,
            )
        scale = lax.rsqrt(squares * (1.0 / D) + 1e-06)
        gate = gate * scale
        act = (gate * jax.nn.sigmoid(gate) * (up * scale)).astype(BF16)
        own = jnp.where(iota((128, EXPERTS), 1) == i // 8, logits, 0.0)
        affinity = jax.nn.sigmoid(jnp.sum(own, axis=1, keepdims=True) * scale)
        high = affinity.astype(BF16).astype(F32)
        lanes = iota((128, 128), 1)
        extra = jnp.where(lanes == 0, high, jnp.where(lanes == 1, affinity - high, 0.0))
        aff_v[...] = jnp.broadcast_to(affinity, (128, 128))
        near_extra = extra[FAR_ROWS:].reshape(2 * NEAR, ROWS, 128).astype(BF16)
        far_out[:, :, CH:] = (4.0 * extra[:FAR_ROWS]).reshape(FAR_SLOTS, ROWS, 128).astype(BF16)

        for k in (2, 1, 3, 0):
            yk = y_at(k)
            cols = pl.ds(pl.multiple_of(yk * CH, 128), CH)
            piece = jnp.dot(act, down_v[half, :, cols], preferred_element_type=F32)
            sb[yk] = piece[:FAR_ROWS].reshape(FAR, 16, CH).astype(BF16)
            weighted = piece[FAR_ROWS:] * affinity[FAR_ROWS:]
            near_out[yk, :, :, :CH] = weighted.reshape(2 * NEAR, ROWS, CH).astype(BF16)
            near_out[yk, :, :, CH:] = near_extra
        for n in range(FAR):
            for k in (2, 1, 3):
                remote(
                    sb.at[y_at(k), n], rb.at[half, y, n], r_send.at[n, k],
                    r_recv.at[half, y, n], s, base4 + y_at(k),
                ).start()
        for n in range(FAR, len(AWAY)):
            for xf, k, m in sends(n):
                pair = 2 * (n - FAR) + xf
                remote(
                    near_out.at[y_at(k), pair], ro.at[FAR_SLOTS + pair * 4 + y],
                    n_send.at[m - FAR_SLOTS], c_recv.at[FAR_SLOTS + pair * 4 + y],
                    holder, column(xf, AWAY[n]) + y_at(k),
                ).start()
        for n in range(FAR):
            total = sb[y, n].astype(F32)
            for k in (1, 3, 2):
                wait_for(rb.at[half, y_at(k), n], r_recv.at[half, y_at(k), n])
                total = total + rb[half, y_at(k), n].astype(F32)
            total = total * aff_v[16 * n : 16 * n + 16, :1]
            far_out[2 * n : 2 * n + 2, :, :CH] = total.reshape(2, ROWS, CH).astype(BF16)
            for xf, k, m in sends(n):
                remote(
                    far_out.at[m], ro.at[m], c_send.at[m], c_recv.at[m],
                    holder, column(xf, AWAY[n]) + y,
                ).start()

        for n in range(FAR):
            for k in range(1, 4):
                wait_for(xb.at[half, y, n], g_send.at[n, k])
                wait_for(sb.at[0, 0], r_send.at[n, k])
        for m in range(FAR_SLOTS):
            wait_for(far_out.at[m], c_send.at[m])
        for m in range(SLOTS - FAR_SLOTS):
            wait_for(near_out.at[0, 0], n_send.at[m])

    def holder_of(step):
        return jnp.where(jnp.logical_and(step > 1, step < 6), SECOND, FIRST)

    def one_step(step, carry):
        pl.when(s == holder_of(step))(lambda: holder_step(step))

        @pl.when(jnp.logical_and(is_second, step == 1))
        def _():
            for sec in range(4):
                gather_routes(sec)
            make_all()

        pl.when(s == live_of(step))(lambda: live_step(step // 4, holder_of(step + 1)))
        return carry

    lax.fori_loop(0, STEPS, one_step, 0)
    pl.when(is_second)(wait_dispatch)

    @pl.when(is_first)
    def _():
        combine(STEPS - 1)
        fin_out[...] = x_v[...].astype(BF16)

        def send_last(k):
            remote(fin_out, fin_in, f_send.at[k], f_recv, y, base4 + y_at(k)).start()

        for k in (2, 1, 3):
            send_last(k)
        pl.when(y != FIRST)(lambda: send_last(0))

        @pl.when(y == FIRST)
        def _():
            pltpu.make_async_copy(fin_out, fin_in, f_recv).start()

    wait_for(fin_in, f_recv)
    pick = (iota((8, SET), 1) == 4 * y + iota((8, SET), 0)).astype(BF16)
    picked = jnp.dot(pick, fin_in[...], preferred_element_type=F32)
    out_ref[...] = picked[:4].astype(BF16)

    @pl.when(is_first)
    def _():
        wait_dispatch()
        for k in range(1, 4):
            wait_for(fin_out, f_send.at[k])
            wait_for(hx_out.at[0], hx_send.at[k])
        pl.when(y != FIRST)(lambda: wait_for(fin_out, f_send.at[0]))

    for n, holder in enumerate((FIRST, SECOND)):
        for k in range(1, 4):
            wait_for(rt_out, rt_send.at[n, k])
        pl.when(s != holder)(lambda: wait_for(rt_out, rt_send.at[n, 0]))


def shards(hidden_in, routes, norm_gain, router_weight, gate_weight, up_weight, down_weight):
    routes = jnp.swapaxes(routes, 3, 4)
    router_weight = jnp.swapaxes(router_weight, 2, 3)
    dma = pltpu.SemaphoreType.DMA
    in_hbm = pl.BlockSpec(memory_space=pltpu.HBM)
    out = pl.pallas_call(
        kernel,
        out_shape=jax.ShapeDtypeStruct((4, CH), BF16),
        in_specs=[in_hbm] * 7,
        out_specs=pl.BlockSpec(memory_space=pltpu.VMEM),
        scratch_shapes=[
            pltpu.VMEM(hidden_in.shape, BF16),
            pltpu.VMEM(routes.shape, jnp.int32),
            pltpu.VMEM(norm_gain.shape, F32),
            pltpu.VMEM(router_weight.shape, BF16),
            pltpu.VMEM((2, D, HID), BF16),
            pltpu.VMEM((2, D, HID), BF16),
            pltpu.VMEM((2, HID, D), BF16),
            pltpu.VMEM((SET, 128), F32),
            pltpu.VMEM((4, 4, SET, 128), F32),
            pltpu.VMEM((4, SET, 128), F32),
            pltpu.VMEM((4, SET, CH), BF16),
            pltpu.VMEM((4, SET, CH), BF16),
            pltpu.VMEM((STEPS, SET, EXPERTS * ROWS), BF16),
            pltpu.VMEM((STEPS, SET, SLOTS * ROWS), BF16),
            pltpu.VMEM((SET, CH), F32),
            pltpu.VMEM((SET, CH), BF16),
            pltpu.VMEM((SET, CH), BF16),
            pltpu.VMEM((EXPERTS, ROWS, CH), BF16),
            pltpu.VMEM((2, 4, len(AWAY), 2, ROWS, CH), BF16),
            pltpu.VMEM((4, FAR, 16, CH), BF16),
            pltpu.VMEM((2, 4, FAR, 16, CH), BF16),
            pltpu.VMEM((128, 128), F32),
            pltpu.VMEM((4, 2 * NEAR, ROWS, WIDE), BF16),
            pltpu.VMEM((FAR_SLOTS, ROWS, WIDE), BF16),
            pltpu.VMEM((SLOTS, ROWS, WIDE), BF16),
            pltpu.VMEM((SET, CH), BF16),
            pltpu.VMEM((SET, CH), BF16),
            dma((2,)),
            dma((2, 5)),
            dma((2, 4)),
            dma((4, 4)),
            dma((4,)),
            dma((4,)),
            dma,
            dma,
            dma((SLOTS,)),
            dma((2, 4, len(AWAY))),
            dma((FAR, 4)),
            dma((FAR, 4)),
            dma((2, 4, FAR)),
            dma((8 * NEAR,)),
            dma((FAR_SLOTS,)),
            dma((SLOTS,)),
            dma((4,)),
            dma,
        ],
        compiler_params=pltpu.CompilerParams(
            collective_id=0, has_side_effects=True, vmem_limit_bytes=63 << 20
        ),
    )(hidden_in, routes, norm_gain, router_weight, gate_weight, up_weight, down_weight)
    return out[None]


def solution(mesh):
    return jax.shard_map(
        shards,
        mesh=mesh,
        in_specs=(
            P(None, "expert", None),
            P(None, "section", None, "expert", None),
            P(None, "section", None),
            P(None, "section", None, None),
            P(None, "section", "expert", None, None),
            P(None, "section", "expert", None, None),
            P(None, "section", "expert", None, None),
        ),
        out_specs=P(None, "expert", "section"),
        check_vma=False,
    )
```

```python
import jax
import jax.numpy as jnp
from jax import lax
from jax.experimental import pallas as pl
from jax.experimental.pallas import tpu as pltpu
from jax.sharding import PartitionSpec as P

MESH = pl.DeviceIdType.MESH
F32 = jnp.float32
BF16 = jnp.bfloat16

D = 3584
CH = 896
WIDE = CH + 128
HID = 256
EXPERTS = 8
ROWS = 8
SET = 16
STEPS = 8
FIRST = 3
SECOND = 0
AWAY = (4, 3, -3, 2, -2, 1, -1, 0)
FAR = 3
NEAR = len(AWAY) - FAR
FAR_SLOTS = 2 * FAR
SLOTS = FAR_SLOTS + 8 * NEAR
FAR_ROWS = 16 * FAR


def remote(src, dst, send, recv, section, expert):
    return pltpu.make_async_remote_copy(
        src_ref=src,
        dst_ref=dst,
        send_sem=send,
        recv_sem=recv,
        device_id=(section, expert),
        device_id_type=MESH,
    )


def wait_for(ref, sem):
    pltpu.make_async_copy(ref, ref, sem).wait()


def iota(shape, dim):
    return lax.broadcasted_iota(jnp.int32, shape, dim)


def kernel(
    hidden_hbm, routes_hbm, gain_hbm, router_hbm, gate_hbm, up_hbm, down_hbm, out_ref,
    hid_v, routes_v, gain_v, router_v, gate_v, up_v, down_v,
    rt_out, rt_in, rsum, hx_out, hx_in, place_pt, far_pt, near_pt, x_v, x_out, x_in, disp, xb,
    own_router, sb, rb, near_out, far_out, ro, fin_out, fin_in,
    in_sem, w_sem, rt_send, rt_recv, hx_send, hx_recv, x_send, x_recv, d_send, a_recv,
    g_send, r_send, r_recv, n_send, c_send, c_recv, f_send, f_recv,
):
    s = lax.axis_index("section")
    i = lax.axis_index("expert")
    xh = i // 32
    z = (i // 4) % 8
    y = i % 4
    base4 = i - y
    is_first = s == FIRST
    is_second = s == SECOND

    def y_at(k):
        return (y + k) % 4

    def column(xf, away):
        return ((xh + xf) % 2) * 32 + ((z + away + 8) % 8) * 4

    def expert_at(xf, away):
        return ((xh + xf) % 2) * 4 + ((z + away + 8) % 8) // 2

    small = [
        pltpu.make_async_copy(hidden_hbm, hid_v, in_sem.at[0]),
        pltpu.make_async_copy(routes_hbm, routes_v, in_sem.at[1]),
    ]
    for copy in small:
        copy.start()

    def weights(c):
        return [
            pltpu.make_async_copy(gain_hbm.at[c], gain_v.at[c], w_sem.at[c, 0]),
            pltpu.make_async_copy(router_hbm.at[c], router_v.at[c], w_sem.at[c, 1]),
            pltpu.make_async_copy(gate_hbm.at[c, 0, 0], gate_v.at[c], w_sem.at[c, 2]),
            pltpu.make_async_copy(up_hbm.at[c, 0, 0], up_v.at[c], w_sem.at[c, 3]),
            pltpu.make_async_copy(down_hbm.at[c, 0, 0], down_v.at[c], w_sem.at[c, 4]),
        ]

    for c in range(2):
        for copy in weights(c):
            copy.start()

    ro[:, :, CH:] = jnp.zeros((SLOTS, ROWS, 128), BF16)

    barrier = pltpu.get_barrier_semaphore()

    def greet(section, expert):
        pl.semaphore_signal(barrier, inc=1, device_id=(section, expert), device_id_type=MESH)

    def greet_all(section, sign):
        for n, away in enumerate(AWAY):
            for xf in range(2):
                for k in range(1 if n < FAR else 4):
                    greet(section, column(xf, sign * away) + y_at(k))

    for k in range(1, 4):
        greet(s, base4 + y_at(k))
    pl.when(s != FIRST)(lambda: greet_all(FIRST, 1))
    pl.when(s != SECOND)(lambda: greet_all(SECOND, 1))
    pairs = 2 * FAR + 8 * NEAR

    @pl.when(jnp.logical_or(is_first, is_second))
    def _():
        lowest = jnp.where(is_first, 0, 1)
        for n in range(3):
            greet_all(lowest + n, -1)
        pl.semaphore_wait(barrier, 3 + 4 * pairs)

    @pl.when(jnp.logical_not(jnp.logical_or(is_first, is_second)))
    def _():
        pl.semaphore_wait(barrier, 3 + 2 * pairs)

    for copy in small:
        copy.wait()
    place = (iota((SET, 4), 0) == 4 * y + iota((SET, 4), 1)).astype(BF16)

    @pl.when(is_first)
    def _():
        placed = jnp.dot(place, hid_v[0], preferred_element_type=F32).astype(BF16)
        for k in range(4):
            hx_out[k] = placed[:, k * CH : (k + 1) * CH]
        for k in (2, 1, 3):
            remote(
                hx_out.at[y_at(k)], hx_in.at[y], hx_send.at[k], hx_recv.at[y],
                s, base4 + y_at(k),
            ).start()

    lane = iota((4, 128), 1)
    diagonal = iota((4, 4), 0) == iota((4, 4), 1)
    tile = jnp.zeros((4, 128), F32)
    for c in range(2):
        chosen = routes_v[c, 0, 0].astype(F32)
        for k in range(2):
            column_k = jnp.sum(jnp.where(diagonal, chosen[k : k + 1], 0.0), axis=1, keepdims=True)
            tile = tile + jnp.where(lane == 2 * c + k, column_k, 0.0)
    rt_out[...] = jnp.dot(place, tile.astype(BF16), preferred_element_type=F32)

    def send_routes(n, holder, k):
        remote(
            rt_out, rt_in.at[s, y], rt_send.at[n, k], rt_recv.at[s, y],
            holder, base4 + y_at(k),
        ).start()

    for n, holder in enumerate((FIRST, SECOND)):
        for k in range(1, 4):
            send_routes(n, holder, k)
        pl.when(s != holder)(lambda: send_routes(n, holder, 0))
        @pl.when(s == holder)
        def _():
            rt_in[holder, y] = rt_out[...]

    def gather_routes(sec):
        for k in range(1, 4):
            wait_for(rt_in.at[sec, y_at(k)], rt_recv.at[sec, y_at(k)])
        pl.when(s != sec)(lambda: wait_for(rt_in.at[sec, y], rt_recv.at[sec, y]))
        total = jnp.zeros((SET, 128), F32)
        for k in range(4):
            total = total + rt_in[sec, k]
        rsum[sec] = total

    def live_of(step):
        return jnp.where(step < 4, step, 7 - step)

    def placement(step, expert, row):
        half = step // 4
        routes = rsum[live_of(step)]
        lanes = iota((SET, 128), 1)
        one = jnp.sum(jnp.where(lanes == 2 * half, routes, 0.0), axis=1, keepdims=True)
        two = jnp.sum(jnp.where(lanes == 2 * half + 1, routes, 0.0), axis=1, keepdims=True)
        expert = expert.astype(F32)
        named = jnp.logical_or(one == expert, two == expert)
        onehot = jnp.where(named, 1.0, 0.0)
        token = iota((SET, SET), 0)
        other = iota((SET, SET), 1)
        earlier = jnp.logical_and(token // 4 == other // 4, other < token)
        count = jnp.dot(
            jnp.where(earlier, 1.0, 0.0).astype(BF16), onehot.astype(BF16),
            preferred_element_type=F32,
        )
        fits = jnp.logical_and(
            count == (row % 2).astype(F32), row // 2 == iota(row.shape, 0) // 4
        )
        return jnp.where(jnp.logical_and(named, fits), 1.0, 0.0).astype(BF16)

    def make_place(step):
        at = iota((SET, EXPERTS * ROWS), 1)
        place_pt[step] = placement(step, at // ROWS, at % ROWS)

    def make_mix(step, first, count):
        at = iota((SET, count * ROWS), 1)
        slot = first + at // ROWS
        near = slot >= FAR_SLOTS
        pair = jnp.where(near, FAR_SLOTS + (slot - FAR_SLOTS) // 4, slot)
        n = pair // 2
        away = jnp.zeros(at.shape, jnp.int32)
        for m, value in enumerate(AWAY):
            away = jnp.where(n == m, value, away)
        expert = ((xh + pair % 2) % 2) * 4 + ((z - away + 8) % 8) // 2
        return placement(step, expert, at % ROWS)

    def make_all():
        def body(step, carry):
            make_place(step)
            far_pt[step] = make_mix(step, 0, FAR_SLOTS)
            near_pt[step] = make_mix(step, FAR_SLOTS, SLOTS - FAR_SLOTS)
            return carry

        lax.fori_loop(0, STEPS, body, 0)

    @pl.when(is_first)
    def _():
        gather_routes(0)
        make_place(0)
        for k in range(1, 4):
            wait_for(hx_in.at[y_at(k)], hx_recv.at[y_at(k)])
        hx_in[y] = hx_out[y]
        x = jnp.zeros((SET, CH), F32)
        for k in range(4):
            x = x + hx_in[k].astype(F32)
        x_v[...] = x

    def combine(step):
        widths = [WIDE] * FAR_SLOTS + [WIDE, CH, CH, CH] * (2 * NEAR)
        mixed = jnp.zeros((SET, WIDE), F32)
        for matrix, first, last in ((near_pt, FAR_SLOTS, SLOTS), (far_pt, 0, FAR_SLOTS)):
            for k in range(first, last):
                wait_for(ro.at[k, :, pl.ds(0, widths[k])], c_recv.at[k])
            rows = ro[first:last].astype(F32).reshape((last - first) * ROWS, WIDE).astype(BF16)
            mixed = mixed + jnp.dot(matrix[step], rows, preferred_element_type=F32)
        weight = mixed[:, CH : CH + 1] + mixed[:, CH + 1 : CH + 2]
        fresh = x_v[...] + 20.0 * mixed[:, :CH] / weight
        x_v[...] = fresh.astype(BF16).astype(F32)

    def sends(n):
        if n < FAR:
            return [(xf, 0, 2 * n + xf) for xf in (1, 0)]
        return [
            (xf, k, FAR_SLOTS + (2 * (n - FAR) + xf) * 4 + k) for k in (2, 1, 3, 0) for xf in (1, 0)
        ]

    def wait_dispatch():
        for m in range(SLOTS):
            wait_for(disp.at[0], d_send.at[m])

    def holder_step(step):
        half = step // 4

        @pl.when(jnp.logical_or(step == 2, step == 6))
        def _():
            wait_for(x_in, x_recv)
            x_v[...] = x_in[...].astype(F32)

        pl.when(step > 0)(lambda: combine(step - 1))
        pl.when(jnp.logical_and(step != 0, step != 2))(wait_dispatch)
        x_out[...] = x_v[...].astype(BF16)
        rows = lax.dot_general(
            place_pt[step], x_out[...], (((0,), (0,)), ((), ())), preferred_element_type=F32
        )
        disp[...] = rows.reshape(EXPERTS, ROWS, CH).astype(BF16)
        order = [(n,) + t for n in range(FAR) for t in sends(n)]
        near = [(n,) + t for n in range(FAR, len(AWAY)) for t in sends(n)]
        order += sorted(near, key=lambda t: (2, 1, 3, 0).index(t[2]))
        for n, xf, k, m in order:
            away = AWAY[n]
            remote(
                disp.at[expert_at(xf, -away)], xb.at[half, y, n, xf],
                d_send.at[m], a_recv.at[half, y, n],
                live_of(step), column(xf, -away) + y_at(k),
            ).start()

        @pl.when(jnp.logical_or(step == 1, step == 5))
        def _():
            handed = remote(x_out, x_in, x_send, x_recv, FIRST + SECOND - s, i)
            handed.start()
            handed.wait_send()

        @pl.when(step == 0)
        def _():
            for sec in range(1, 4):
                gather_routes(sec)
            make_all()

    def live_step(half, holder):
        for copy in weights(half):
            copy.wait()
        own = iota((EXPERTS, D), 0) == i // 8
        own_router[...] = jnp.sum(
            jnp.where(own, router_v[half, 0].astype(F32), 0.0), axis=0, keepdims=True
        )
        for n in reversed(range(FAR)):
            rows = xb.at[half, y, n]
            wait_for(rows, a_recv.at[half, y, n])
            for k in (2, 1, 3):
                remote(
                    rows, rows, g_send.at[n, k], a_recv.at[half, y, n], s, base4 + y_at(k)
                ).start()
        def hidden(first, last):
            count = 16 * (last - first)
            gate = jnp.zeros((count, HID), F32)
            up = jnp.zeros((count, HID), F32)
            logits = jnp.zeros((count, 1), F32)
            squares = jnp.zeros((count, 1), F32)
            for k in (0, 1, 3, 2):
                yk = y_at(k)
                for n in range(first, last):
                    if k > 0 or n >= FAR:
                        wait_for(xb.at[half, yk, n], a_recv.at[half, yk, n])
                rows = xb[half, yk, first:last].astype(F32).reshape(count, CH)
                squares = squares + jnp.sum(rows * rows, axis=1, keepdims=True)
                depth = pl.ds(pl.multiple_of(yk * CH, 128), CH)
                scaled = (rows * gain_v[half, :, depth]).astype(BF16)
                gate = gate + jnp.dot(scaled, gate_v[half, depth, :], preferred_element_type=F32)
                up = up + jnp.dot(scaled, up_v[half, depth, :], preferred_element_type=F32)
                logits = logits + jnp.sum(
                    scaled.astype(F32) * own_router[:, depth], axis=1, keepdims=True
                )
            scale = lax.rsqrt(squares * (1.0 / D) + 1e-06)
            gate = gate * scale
            act = (gate * jax.nn.sigmoid(gate) * (up * scale)).astype(BF16)
            affinity = jax.nn.sigmoid(logits * scale)
            high = affinity.astype(BF16).astype(F32)
            lanes = iota((count, 128), 1)
            extra = jnp.where(lanes == 0, high, jnp.where(lanes == 1, affinity - high, 0.0))
            return act, affinity, extra

        def piece_of(act, yk):
            cols = pl.ds(pl.multiple_of(yk * CH, 128), CH)
            return jnp.dot(act, down_v[half, :, cols], preferred_element_type=F32)

        act, affinity, extra = hidden(FAR, len(AWAY))
        near_out[y, :, :, CH:] = (4.0 * extra).reshape(2 * NEAR, ROWS, 128).astype(BF16)
        for k in (2, 1, 3, 0):
            yk = y_at(k)
            weighted = piece_of(act, yk) * affinity
            near_out[yk, :, :, :CH] = weighted.reshape(2 * NEAR, ROWS, CH).astype(BF16)
            for n in range(FAR, len(AWAY)):
                for xf in (1, 0):
                    pair = 2 * (n - FAR) + xf
                    width = pl.ds(0, WIDE if k == 0 else CH)
                    remote(
                        near_out.at[yk, pair, :, width],
                        ro.at[FAR_SLOTS + pair * 4 + k, :, width],
                        n_send.at[pair * 4 + k], c_recv.at[FAR_SLOTS + pair * 4 + k],
                        holder, column(xf, AWAY[n]) + yk,
                    ).start()

        act, affinity, extra = hidden(0, FAR)
        far_out[:, :, CH:] = (4.0 * extra).reshape(FAR_SLOTS, ROWS, 128).astype(BF16)
        for k in (2, 1, 3, 0):
            yk = y_at(k)
            sb[yk] = piece_of(act, yk).reshape(FAR, 16, CH).astype(BF16)
            if k > 0:
                for n in range(FAR):
                    remote(
                        sb.at[yk, n], rb.at[half, y, n], r_send.at[n, k],
                        r_recv.at[half, y, n], s, base4 + yk,
                    ).start()
        for n in range(FAR):
            total = sb[y, n].astype(F32)
            for k in (1, 3, 2):
                wait_for(rb.at[half, y_at(k), n], r_recv.at[half, y_at(k), n])
                total = total + rb[half, y_at(k), n].astype(F32)
            total = total * affinity[16 * n : 16 * n + 16]
            far_out[2 * n : 2 * n + 2, :, :CH] = total.reshape(2, ROWS, CH).astype(BF16)
            for xf, k, m in sends(n):
                remote(
                    far_out.at[m], ro.at[m], c_send.at[m], c_recv.at[m],
                    holder, column(xf, AWAY[n]) + y,
                ).start()

        for n in range(FAR):
            for k in range(1, 4):
                wait_for(xb.at[half, y, n], g_send.at[n, k])
                wait_for(sb.at[0, 0], r_send.at[n, k])
        for m in range(FAR_SLOTS):
            wait_for(far_out.at[m], c_send.at[m])
        for m in range(SLOTS - FAR_SLOTS):
            wait_for(near_out.at[0, 0, :, pl.ds(0, CH if m % 4 else WIDE)], n_send.at[m])

    def holder_of(step):
        return jnp.where(jnp.logical_and(step > 1, step < 6), SECOND, FIRST)

    def one_step(step, carry):
        pl.when(s == holder_of(step))(lambda: holder_step(step))

        @pl.when(jnp.logical_and(is_second, step == 1))
        def _():
            for sec in range(4):
                gather_routes(sec)
            make_all()

        pl.when(s == live_of(step))(lambda: live_step(step // 4, holder_of(step + 1)))
        return carry

    lax.fori_loop(0, STEPS, one_step, 0)
    pl.when(is_second)(wait_dispatch)

    @pl.when(is_first)
    def _():
        combine(STEPS - 1)
        fin_out[...] = x_v[...].astype(BF16)

        def send_last(k):
            remote(fin_out, fin_in, f_send.at[k], f_recv, y, base4 + y_at(k)).start()

        for k in (2, 1, 3):
            send_last(k)
        pl.when(y != FIRST)(lambda: send_last(0))

        @pl.when(y == FIRST)
        def _():
            pltpu.make_async_copy(fin_out, fin_in, f_recv).start()

    wait_for(fin_in, f_recv)
    pick = (iota((8, SET), 1) == 4 * y + iota((8, SET), 0)).astype(BF16)
    picked = jnp.dot(pick, fin_in[...], preferred_element_type=F32)
    out_ref[...] = picked[:4].astype(BF16)

    @pl.when(is_first)
    def _():
        wait_dispatch()
        for k in range(1, 4):
            wait_for(fin_out, f_send.at[k])
            wait_for(hx_out.at[0], hx_send.at[k])
        pl.when(y != FIRST)(lambda: wait_for(fin_out, f_send.at[0]))

    for n, holder in enumerate((FIRST, SECOND)):
        for k in range(1, 4):
            wait_for(rt_out, rt_send.at[n, k])
        pl.when(s != holder)(lambda: wait_for(rt_out, rt_send.at[n, 0]))


def shards(hidden_in, routes, norm_gain, router_weight, gate_weight, up_weight, down_weight):
    routes = jnp.swapaxes(routes, 3, 4)
    router_weight = jnp.swapaxes(router_weight, 2, 3)
    dma = pltpu.SemaphoreType.DMA
    in_hbm = pl.BlockSpec(memory_space=pltpu.HBM)
    out = pl.pallas_call(
        kernel,
        out_shape=jax.ShapeDtypeStruct((4, CH), BF16),
        in_specs=[in_hbm] * 7,
        out_specs=pl.BlockSpec(memory_space=pltpu.VMEM),
        scratch_shapes=[
            pltpu.VMEM(hidden_in.shape, BF16),
            pltpu.VMEM(routes.shape, jnp.int32),
            pltpu.VMEM(norm_gain.shape, F32),
            pltpu.VMEM(router_weight.shape, BF16),
            pltpu.VMEM((2, D, HID), BF16),
            pltpu.VMEM((2, D, HID), BF16),
            pltpu.VMEM((2, HID, D), BF16),
            pltpu.VMEM((SET, 128), F32),
            pltpu.VMEM((4, 4, SET, 128), F32),
            pltpu.VMEM((4, SET, 128), F32),
            pltpu.VMEM((4, SET, CH), BF16),
            pltpu.VMEM((4, SET, CH), BF16),
            pltpu.VMEM((STEPS, SET, EXPERTS * ROWS), BF16),
            pltpu.VMEM((STEPS, SET, FAR_SLOTS * ROWS), BF16),
            pltpu.VMEM((STEPS, SET, (SLOTS - FAR_SLOTS) * ROWS), BF16),
            pltpu.VMEM((SET, CH), F32),
            pltpu.VMEM((SET, CH), BF16),
            pltpu.VMEM((SET, CH), BF16),
            pltpu.VMEM((EXPERTS, ROWS, CH), BF16),
            pltpu.VMEM((2, 4, len(AWAY), 2, ROWS, CH), BF16),
            pltpu.VMEM((1, D), F32),
            pltpu.VMEM((4, FAR, 16, CH), BF16),
            pltpu.VMEM((2, 4, FAR, 16, CH), BF16),
            pltpu.VMEM((4, 2 * NEAR, ROWS, WIDE), BF16),
            pltpu.VMEM((FAR_SLOTS, ROWS, WIDE), BF16),
            pltpu.VMEM((SLOTS, ROWS, WIDE), BF16),
            pltpu.VMEM((SET, CH), BF16),
            pltpu.VMEM((SET, CH), BF16),
            dma((2,)),
            dma((2, 5)),
            dma((2, 4)),
            dma((4, 4)),
            dma((4,)),
            dma((4,)),
            dma,
            dma,
            dma((SLOTS,)),
            dma((2, 4, len(AWAY))),
            dma((FAR, 4)),
            dma((FAR, 4)),
            dma((2, 4, FAR)),
            dma((8 * NEAR,)),
            dma((FAR_SLOTS,)),
            dma((SLOTS,)),
            dma((4,)),
            dma,
        ],
        compiler_params=pltpu.CompilerParams(
            collective_id=0, has_side_effects=True, vmem_limit_bytes=63 << 20
        ),
    )(hidden_in, routes, norm_gain, router_weight, gate_weight, up_weight, down_weight)
    return out[None]


def solution(mesh):
    return jax.shard_map(
        shards,
        mesh=mesh,
        in_specs=(
            P(None, "expert", None),
            P(None, "section", None, "expert", None),
            P(None, "section", None),
            P(None, "section", None, None),
            P(None, "section", "expert", None, None),
            P(None, "section", "expert", None, None),
            P(None, "section", "expert", None, None),
        ),
        out_specs=P(None, "expert", "section"),
        check_vma=False,
    )
```

```python
import jax
import jax.numpy as jnp
from jax import lax
from jax.experimental import pallas as pl
from jax.experimental.pallas import tpu as pltpu
from jax.sharding import PartitionSpec as P

MESH = pl.DeviceIdType.MESH
F32 = jnp.float32
BF16 = jnp.bfloat16

D = 3584
CH = 896
WIDE = CH + 128
HID = 256
EXPERTS = 8
ROWS = 8
SET = 16
STEPS = 8
FIRST = 3
SECOND = 0
AWAY = (4, 3, -3, 2, -2, 1, -1, 0)
FAR = 3
NEAR = len(AWAY) - FAR
FAR_SLOTS = 2 * FAR
SLOTS = FAR_SLOTS + 8 * NEAR
FAR_ROWS = 16 * FAR


def remote(src, dst, send, recv, section, expert):
    return pltpu.make_async_remote_copy(
        src_ref=src,
        dst_ref=dst,
        send_sem=send,
        recv_sem=recv,
        device_id=(section, expert),
        device_id_type=MESH,
    )


def wait_for(ref, sem):
    pltpu.make_async_copy(ref, ref, sem).wait()


def iota(shape, dim):
    return lax.broadcasted_iota(jnp.int32, shape, dim)


def kernel(
    hidden_hbm, routes_hbm, gain_hbm, router_hbm, gate_hbm, up_hbm, down_hbm, out_ref,
    hid_v, routes_v, gain_v, router_v, gate_v, up_v, down_v,
    rt_out, rt_in, rsum, hx_out, hx_in, place_pt, far_pt, near_pt, x_v, x_out, x_in, disp, xb,
    own_router, sb, rb, near_out, far_out, ro, fin_out, fin_in,
    in_sem, w_sem, rt_send, rt_recv, hx_send, hx_recv, x_send, x_recv, d_send, a_recv,
    g_send, r_send, r_recv, n_send, c_send, c_recv, f_send, f_recv,
):
    s = lax.axis_index("section")
    i = lax.axis_index("expert")
    xh = i // 32
    z = (i // 4) % 8
    y = i % 4
    base4 = i - y
    is_first = s == FIRST
    is_second = s == SECOND

    def y_at(k):
        return (y + k) % 4

    def column(xf, away):
        return ((xh + xf) % 2) * 32 + ((z + away + 8) % 8) * 4

    def expert_at(xf, away):
        return ((xh + xf) % 2) * 4 + ((z + away + 8) % 8) // 2

    small = [
        pltpu.make_async_copy(hidden_hbm, hid_v, in_sem.at[0]),
        pltpu.make_async_copy(routes_hbm, routes_v, in_sem.at[1]),
    ]
    for copy in small:
        copy.start()

    def weights(c):
        return [
            pltpu.make_async_copy(gain_hbm.at[c], gain_v.at[c], w_sem.at[c, 0]),
            pltpu.make_async_copy(router_hbm.at[c], router_v.at[c], w_sem.at[c, 1]),
            pltpu.make_async_copy(gate_hbm.at[c, 0, 0], gate_v.at[c], w_sem.at[c, 2]),
            pltpu.make_async_copy(up_hbm.at[c, 0, 0], up_v.at[c], w_sem.at[c, 3]),
            pltpu.make_async_copy(down_hbm.at[c, 0, 0], down_v.at[c], w_sem.at[c, 4]),
        ]

    for c in range(2):
        for copy in weights(c):
            copy.start()

    ro[:, :, CH:] = jnp.zeros((SLOTS, ROWS, 128), BF16)

    barrier = pltpu.get_barrier_semaphore()

    def greet(section, expert):
        pl.semaphore_signal(barrier, inc=1, device_id=(section, expert), device_id_type=MESH)

    def greet_all(section, sign):
        for n, away in enumerate(AWAY):
            for xf in range(2):
                for k in range(1 if n < FAR else 4):
                    greet(section, column(xf, sign * away) + y_at(k))

    for k in range(1, 4):
        greet(s, base4 + y_at(k))
    pl.when(s != FIRST)(lambda: greet_all(FIRST, 1))
    pl.when(s != SECOND)(lambda: greet_all(SECOND, 1))
    pairs = 2 * FAR + 8 * NEAR

    @pl.when(jnp.logical_or(is_first, is_second))
    def _():
        lowest = jnp.where(is_first, 0, 1)
        for n in range(3):
            greet_all(lowest + n, -1)

    for copy in small:
        copy.wait()
    place = (iota((SET, 4), 0) == 4 * y + iota((SET, 4), 1)).astype(BF16)

    @pl.when(is_first)
    def _():
        placed = jnp.dot(place, hid_v[0], preferred_element_type=F32).astype(BF16)
        for k in range(4):
            hx_out[k] = placed[:, k * CH : (k + 1) * CH]

    lane = iota((4, 128), 1)
    diagonal = iota((4, 4), 0) == iota((4, 4), 1)
    tile = jnp.zeros((4, 128), F32)
    for c in range(2):
        chosen = routes_v[c, 0, 0].astype(F32)
        for k in range(2):
            column_k = jnp.sum(jnp.where(diagonal, chosen[k : k + 1], 0.0), axis=1, keepdims=True)
            tile = tile + jnp.where(lane == 2 * c + k, column_k, 0.0)
    rt_out[...] = jnp.dot(place, tile.astype(BF16), preferred_element_type=F32)

    pl.semaphore_wait(barrier, 3 + jnp.where(jnp.logical_or(is_first, is_second), 4, 2) * pairs)

    @pl.when(is_first)
    def _():
        for k in (2, 1, 3):
            remote(
                hx_out.at[y_at(k)], hx_in.at[y], hx_send.at[k], hx_recv.at[y],
                s, base4 + y_at(k),
            ).start()

    def send_routes(n, holder, k):
        remote(
            rt_out, rt_in.at[s, y], rt_send.at[n, k], rt_recv.at[s, y],
            holder, base4 + y_at(k),
        ).start()

    for n, holder in enumerate((FIRST, SECOND)):
        for k in range(1, 4):
            send_routes(n, holder, k)
        pl.when(s != holder)(lambda: send_routes(n, holder, 0))
        @pl.when(s == holder)
        def _():
            rt_in[holder, y] = rt_out[...]

    def gather_routes(sec):
        for k in range(1, 4):
            wait_for(rt_in.at[sec, y_at(k)], rt_recv.at[sec, y_at(k)])
        pl.when(s != sec)(lambda: wait_for(rt_in.at[sec, y], rt_recv.at[sec, y]))
        total = jnp.zeros((SET, 128), F32)
        for k in range(4):
            total = total + rt_in[sec, k]
        rsum[sec] = total

    def live_of(step):
        return jnp.where(step < 4, step, 7 - step)

    def placement(step, expert, row):
        half = step // 4
        routes = rsum[live_of(step)]
        lanes = iota((SET, 128), 1)
        one = jnp.sum(jnp.where(lanes == 2 * half, routes, 0.0), axis=1, keepdims=True)
        two = jnp.sum(jnp.where(lanes == 2 * half + 1, routes, 0.0), axis=1, keepdims=True)
        expert = expert.astype(F32)
        named = jnp.logical_or(one == expert, two == expert)
        onehot = jnp.where(named, 1.0, 0.0)
        token = iota((SET, SET), 0)
        other = iota((SET, SET), 1)
        earlier = jnp.logical_and(token // 4 == other // 4, other < token)
        count = jnp.dot(
            jnp.where(earlier, 1.0, 0.0).astype(BF16), onehot.astype(BF16),
            preferred_element_type=F32,
        )
        fits = jnp.logical_and(
            count == (row % 2).astype(F32), row // 2 == iota(row.shape, 0) // 4
        )
        return jnp.where(jnp.logical_and(named, fits), 1.0, 0.0).astype(BF16)

    def make_place(step):
        at = iota((SET, EXPERTS * ROWS), 1)
        place_pt[step] = placement(step, at // ROWS, at % ROWS)

    def make_mix(step, first, count):
        at = iota((SET, count * ROWS), 1)
        slot = first + at // ROWS
        near = slot >= FAR_SLOTS
        pair = jnp.where(near, FAR_SLOTS + (slot - FAR_SLOTS) // 4, slot)
        n = pair // 2
        away = jnp.zeros(at.shape, jnp.int32)
        for m, value in enumerate(AWAY):
            away = jnp.where(n == m, value, away)
        expert = ((xh + pair % 2) % 2) * 4 + ((z - away + 8) % 8) // 2
        return placement(step, expert, at % ROWS)

    def make_all():
        def body(step, carry):
            make_place(step)
            far_pt[step] = make_mix(step, 0, FAR_SLOTS)
            near_pt[step] = make_mix(step, FAR_SLOTS, SLOTS - FAR_SLOTS)
            return carry

        lax.fori_loop(0, STEPS, body, 0)

    @pl.when(is_first)
    def _():
        gather_routes(0)
        make_place(0)
        for k in range(1, 4):
            wait_for(hx_in.at[y_at(k)], hx_recv.at[y_at(k)])
        hx_in[y] = hx_out[y]
        x = jnp.zeros((SET, CH), F32)
        for k in range(4):
            x = x + hx_in[k].astype(F32)
        x_v[...] = x

    def combine(step):
        widths = [WIDE] * FAR_SLOTS + [WIDE, CH, CH, CH] * (2 * NEAR)
        mixed = jnp.zeros((SET, WIDE), F32)
        for matrix, first, last in ((near_pt, FAR_SLOTS, SLOTS), (far_pt, 0, FAR_SLOTS)):
            for k in range(first, last):
                wait_for(ro.at[k, :, pl.ds(0, widths[k])], c_recv.at[k])
            rows = ro[first:last].astype(F32).reshape((last - first) * ROWS, WIDE).astype(BF16)
            mixed = mixed + jnp.dot(matrix[step], rows, preferred_element_type=F32)
        weight = mixed[:, CH : CH + 1] + mixed[:, CH + 1 : CH + 2]
        fresh = x_v[...] + 20.0 * mixed[:, :CH] / weight
        x_v[...] = fresh.astype(BF16).astype(F32)

    def sends(n):
        if n < FAR:
            return [(xf, 0, 2 * n + xf) for xf in (1, 0)]
        return [
            (xf, k, FAR_SLOTS + (2 * (n - FAR) + xf) * 4 + k) for k in (2, 1, 3, 0) for xf in (1, 0)
        ]

    def wait_dispatch():
        for m in range(SLOTS):
            wait_for(disp.at[0], d_send.at[m])

    def holder_step(step):
        half = step // 4

        @pl.when(jnp.logical_or(step == 2, step == 6))
        def _():
            wait_for(x_in, x_recv)
            x_v[...] = x_in[...].astype(F32)

        pl.when(jnp.logical_and(step != 0, step != 2))(wait_dispatch)
        pl.when(step > 0)(lambda: combine(step - 1))
        x_out[...] = x_v[...].astype(BF16)
        rows = lax.dot_general(
            place_pt[step], x_out[...], (((0,), (0,)), ((), ())), preferred_element_type=F32
        )
        disp[...] = rows.reshape(EXPERTS, ROWS, CH).astype(BF16)
        order = [(n,) + t for n in range(FAR) for t in sends(n)]
        near = [(n,) + t for n in range(FAR, len(AWAY)) for t in sends(n)]
        order += sorted(near, key=lambda t: (2, 1, 3, 0).index(t[2]))
        for n, xf, k, m in order:
            away = AWAY[n]
            remote(
                disp.at[expert_at(xf, -away)], xb.at[half, y, n, xf],
                d_send.at[m], a_recv.at[half, y, n],
                live_of(step), column(xf, -away) + y_at(k),
            ).start()

        @pl.when(jnp.logical_or(step == 1, step == 5))
        def _():
            handed = remote(x_out, x_in, x_send, x_recv, FIRST + SECOND - s, i)
            handed.start()
            handed.wait_send()

        @pl.when(step == 0)
        def _():
            for sec in range(1, 4):
                gather_routes(sec)
            make_all()

    def live_step(half, holder):
        for copy in weights(half):
            copy.wait()
        own = iota((EXPERTS, D), 0) == i // 8
        own_router[...] = jnp.sum(
            jnp.where(own, router_v[half, 0].astype(F32), 0.0), axis=0, keepdims=True
        )
        for n in reversed(range(FAR)):
            rows = xb.at[half, y, n]
            wait_for(rows, a_recv.at[half, y, n])
            for k in (2, 1, 3):
                remote(
                    rows, rows, g_send.at[n, k], a_recv.at[half, y, n], s, base4 + y_at(k)
                ).start()
        def hidden(first, last):
            count = 16 * (last - first)
            gate = jnp.zeros((count, HID), F32)
            up = jnp.zeros((count, HID), F32)
            logits = jnp.zeros((count, 1), F32)
            squares = jnp.zeros((count, 1), F32)
            for k in (0, 1, 3, 2):
                yk = y_at(k)
                for n in range(first, last):
                    if k > 0 or n >= FAR:
                        wait_for(xb.at[half, yk, n], a_recv.at[half, yk, n])
                rows = xb[half, yk, first:last].astype(F32).reshape(count, CH)
                squares = squares + jnp.sum(rows * rows, axis=1, keepdims=True)
                depth = pl.ds(pl.multiple_of(yk * CH, 128), CH)
                scaled = (rows * gain_v[half, :, depth]).astype(BF16)
                gate = gate + jnp.dot(scaled, gate_v[half, depth, :], preferred_element_type=F32)
                up = up + jnp.dot(scaled, up_v[half, depth, :], preferred_element_type=F32)
                logits = logits + jnp.sum(
                    scaled.astype(F32) * own_router[:, depth], axis=1, keepdims=True
                )
            scale = lax.rsqrt(squares * (1.0 / D) + 1e-06)
            gate = gate * scale
            act = (gate * jax.nn.sigmoid(gate) * (up * scale)).astype(BF16)
            affinity = jax.nn.sigmoid(logits * scale)
            high = affinity.astype(BF16).astype(F32)
            lanes = iota((count, 128), 1)
            extra = jnp.where(lanes == 0, high, jnp.where(lanes == 1, affinity - high, 0.0))
            return act, affinity, extra

        def piece_of(act, yk):
            cols = pl.ds(pl.multiple_of(yk * CH, 128), CH)
            return jnp.dot(act, down_v[half, :, cols], preferred_element_type=F32)

        def send_near(k):
            yk = y_at(k)
            for n in range(FAR, len(AWAY)):
                for xf in (1, 0):
                    pair = 2 * (n - FAR) + xf
                    width = pl.ds(0, WIDE if k == 0 else CH)
                    remote(
                        near_out.at[yk, pair, :, width],
                        ro.at[FAR_SLOTS + pair * 4 + k, :, width],
                        n_send.at[pair * 4 + k], c_recv.at[FAR_SLOTS + pair * 4 + k],
                        holder, column(xf, AWAY[n]) + yk,
                    ).start()

        act, affinity, extra = hidden(FAR, len(AWAY))
        near_out[y, :, :, CH:] = (4.0 * extra).reshape(2 * NEAR, ROWS, 128).astype(BF16)
        for k in (2, 1, 3, 0):
            yk = y_at(k)
            weighted = piece_of(act, yk) * affinity
            near_out[yk, :, :, :CH] = weighted.reshape(2 * NEAR, ROWS, CH).astype(BF16)
            if k in (2,):
                send_near(k)

        act, affinity, extra = hidden(0, FAR)
        far_out[:, :, CH:] = (4.0 * extra).reshape(FAR_SLOTS, ROWS, 128).astype(BF16)
        for k in (2, 1, 3, 0):
            yk = y_at(k)
            sb[yk] = piece_of(act, yk).reshape(FAR, 16, CH).astype(BF16)
            if k > 0:
                for n in range(FAR):
                    remote(
                        sb.at[yk, n], rb.at[half, y, n], r_send.at[n, k],
                        r_recv.at[half, y, n], s, base4 + yk,
                    ).start()
        for k in (1, 3, 0):
            send_near(k)
        for n in range(FAR):
            total = sb[y, n].astype(F32)
            for k in (1, 3, 2):
                wait_for(rb.at[half, y_at(k), n], r_recv.at[half, y_at(k), n])
                total = total + rb[half, y_at(k), n].astype(F32)
            total = total * affinity[16 * n : 16 * n + 16]
            far_out[2 * n : 2 * n + 2, :, :CH] = total.reshape(2, ROWS, CH).astype(BF16)
            for xf, k, m in sends(n):
                remote(
                    far_out.at[m], ro.at[m], c_send.at[m], c_recv.at[m],
                    holder, column(xf, AWAY[n]) + y,
                ).start()

        for n in range(FAR):
            for k in range(1, 4):
                wait_for(xb.at[half, y, n], g_send.at[n, k])
                wait_for(sb.at[0, 0], r_send.at[n, k])
        for m in range(FAR_SLOTS):
            wait_for(far_out.at[m], c_send.at[m])
        for m in range(SLOTS - FAR_SLOTS):
            wait_for(near_out.at[0, 0, :, pl.ds(0, CH if m % 4 else WIDE)], n_send.at[m])

    def holder_of(step):
        return jnp.where(jnp.logical_and(step > 1, step < 6), SECOND, FIRST)

    def one_step(step, carry):
        pl.when(s == holder_of(step))(lambda: holder_step(step))

        @pl.when(jnp.logical_and(is_second, step == 1))
        def _():
            for sec in range(4):
                gather_routes(sec)
            make_all()

        pl.when(s == live_of(step))(lambda: live_step(step // 4, holder_of(step + 1)))
        return carry

    lax.fori_loop(0, STEPS, one_step, 0)
    pl.when(is_second)(wait_dispatch)

    @pl.when(is_first)
    def _():
        combine(STEPS - 1)
        fin_out[...] = x_v[...].astype(BF16)

        def send_last(k):
            remote(fin_out, fin_in, f_send.at[k], f_recv, y, base4 + y_at(k)).start()

        for k in (2, 1, 3):
            send_last(k)
        pl.when(y != FIRST)(lambda: send_last(0))

        @pl.when(y == FIRST)
        def _():
            pltpu.make_async_copy(fin_out, fin_in, f_recv).start()

    wait_for(fin_in, f_recv)
    pick = (iota((8, SET), 1) == 4 * y + iota((8, SET), 0)).astype(BF16)
    picked = jnp.dot(pick, fin_in[...], preferred_element_type=F32)
    out_ref[...] = picked[:4].astype(BF16)

    @pl.when(is_first)
    def _():
        wait_dispatch()
        for k in range(1, 4):
            wait_for(fin_out, f_send.at[k])
            wait_for(hx_out.at[0], hx_send.at[k])
        pl.when(y != FIRST)(lambda: wait_for(fin_out, f_send.at[0]))

    for n, holder in enumerate((FIRST, SECOND)):
        for k in range(1, 4):
            wait_for(rt_out, rt_send.at[n, k])
        pl.when(s != holder)(lambda: wait_for(rt_out, rt_send.at[n, 0]))


def shards(hidden_in, routes, norm_gain, router_weight, gate_weight, up_weight, down_weight):
    routes = jnp.swapaxes(routes, 3, 4)
    router_weight = jnp.swapaxes(router_weight, 2, 3)
    dma = pltpu.SemaphoreType.DMA
    in_hbm = pl.BlockSpec(memory_space=pltpu.HBM)
    out = pl.pallas_call(
        kernel,
        out_shape=jax.ShapeDtypeStruct((4, CH), BF16),
        in_specs=[in_hbm] * 7,
        out_specs=pl.BlockSpec(memory_space=pltpu.VMEM),
        scratch_shapes=[
            pltpu.VMEM(hidden_in.shape, BF16),
            pltpu.VMEM(routes.shape, jnp.int32),
            pltpu.VMEM(norm_gain.shape, F32),
            pltpu.VMEM(router_weight.shape, BF16),
            pltpu.VMEM((2, D, HID), BF16),
            pltpu.VMEM((2, D, HID), BF16),
            pltpu.VMEM((2, HID, D), BF16),
            pltpu.VMEM((SET, 128), F32),
            pltpu.VMEM((4, 4, SET, 128), F32),
            pltpu.VMEM((4, SET, 128), F32),
            pltpu.VMEM((4, SET, CH), BF16),
            pltpu.VMEM((4, SET, CH), BF16),
            pltpu.VMEM((STEPS, SET, EXPERTS * ROWS), BF16),
            pltpu.VMEM((STEPS, SET, FAR_SLOTS * ROWS), BF16),
            pltpu.VMEM((STEPS, SET, (SLOTS - FAR_SLOTS) * ROWS), BF16),
            pltpu.VMEM((SET, CH), F32),
            pltpu.VMEM((SET, CH), BF16),
            pltpu.VMEM((SET, CH), BF16),
            pltpu.VMEM((EXPERTS, ROWS, CH), BF16),
            pltpu.VMEM((2, 4, len(AWAY), 2, ROWS, CH), BF16),
            pltpu.VMEM((1, D), F32),
            pltpu.VMEM((4, FAR, 16, CH), BF16),
            pltpu.VMEM((2, 4, FAR, 16, CH), BF16),
            pltpu.VMEM((4, 2 * NEAR, ROWS, WIDE), BF16),
            pltpu.VMEM((FAR_SLOTS, ROWS, WIDE), BF16),
            pltpu.VMEM((SLOTS, ROWS, WIDE), BF16),
            pltpu.VMEM((SET, CH), BF16),
            pltpu.VMEM((SET, CH), BF16),
            dma((2,)),
            dma((2, 5)),
            dma((2, 4)),
            dma((4, 4)),
            dma((4,)),
            dma((4,)),
            dma,
            dma,
            dma((SLOTS,)),
            dma((2, 4, len(AWAY))),
            dma((FAR, 4)),
            dma((FAR, 4)),
            dma((2, 4, FAR)),
            dma((8 * NEAR,)),
            dma((FAR_SLOTS,)),
            dma((SLOTS,)),
            dma((4,)),
            dma,
        ],
        compiler_params=pltpu.CompilerParams(
            collective_id=0, has_side_effects=True, vmem_limit_bytes=63 << 20
        ),
    )(hidden_in, routes, norm_gain, router_weight, gate_weight, up_weight, down_weight)
    return out[None]


def solution(mesh):
    return jax.shard_map(
        shards,
        mesh=mesh,
        in_specs=(
            P(None, "expert", None),
            P(None, "section", None, "expert", None),
            P(None, "section", None),
            P(None, "section", None, None),
            P(None, "section", "expert", None, None),
            P(None, "section", "expert", None, None),
            P(None, "section", "expert", None, None),
        ),
        out_specs=P(None, "expert", "section"),
        check_vma=False,
    )
```
